32 devices in a mesh: dp: 2 (over x), row: 4 (over y, core), col: 4 (over z).
Axes of the slice: x: 2, y: 2, z: 4, core: 2. Of those that a mesh axis runs over, the one named last changes fastest.
Arguments:
- tokens: bfloat16 [768, 16384], P('col', ('dp', 'row')), may hold values from -6 to 6
- segments: int32 [8, 2048], P('dp'), may hold values from 0 to 7, never falling along the last dimension, each value on 1 to 819 neighbouring positions
- ln1_gain: bfloat16 [768], P('col'), may hold values from 0.3984375 to 1.59375
- ln1_bias: bfloat16 [768], P('col'), may hold values from -1.75 to 1.75
- w_query: bfloat16 [768, 768], P('col', 'row'), may hold values from -0.21875 to 0.21875
- q_bias: bfloat16 [768], P('row'), may hold values from -1.75 to 1.75
- w_key: bfloat16 [768, 768], P('col', 'row'), may hold values from -0.21875 to 0.21875
- w_value: bfloat16 [768, 768], P('col', 'row'), may hold values from -0.21875 to 0.21875
- v_bias: bfloat16 [768], P('row'), may hold values from -1.75 to 1.75
- w_out: bfloat16 [768, 768], P('row', 'col'), may hold values from -1.75 to 1.75
- out_bias: bfloat16 [768], P('col'), may hold values from -1.75 to 1.75
- ln2_gain: bfloat16 [768], P('col'), may hold values from 0.3984375 to 1.59375
- ln2_bias: bfloat16 [768], P('col'), may hold values from -1.75 to 1.75
- w_up: bfloat16 [768, 3072], P('col', 'row'), may hold values from -0.21875 to 0.21875
- up_bias: bfloat16 [3072], P('row'), may hold values from -1.75 to 1.75
- w_down: bfloat16 [768, 3072], P('col', 'row'), may hold values from -0.109375 to 0.109375
- down_bias: bfloat16 [768], P('col'), may hold values from -1.75 to 1.75
- cotangent: bfloat16 [768, 16384], P('col', ('dp', 'row')), may hold values from -6 to 6
Outputs:
- out: bfloat16 [768, 16384], P('col', ('dp', 'row'))
- grad_tokens: float32 [768, 16384], P('col', ('dp', 'row'))
- grad_ln1_gain: float32 [768], P('col')
- grad_ln1_bias: float32 [768], P('col')
- grad_w_query: float32 [768, 768], P('col', 'row')
- grad_q_bias: float32 [768], P('row')
- grad_w_key: float32 [768, 768], P('col', 'row')
- grad_w_value: float32 [768, 768], P('col', 'row')
- grad_v_bias: float32 [768], P('row')
- grad_w_out: float32 [768, 768], P('row', 'col')
- grad_out_bias: float32 [768], P('col')
- grad_ln2_gain: float32 [768], P('col')
- grad_ln2_bias: float32 [768], P('col')
- grad_w_up: float32 [768, 3072], P('col', 'row')
- grad_up_bias: float32 [3072], P('row')
- grad_w_down: float32 [768, 3072], P('col', 'row')
- grad_down_bias: float32 [768], P('col')
The draws below stay inside these ranges and needn't reach their ends.
Inputs may be any that keep to these rules, and one draw needn't show every extreme that they name: `segments`: numbers never fall along a sequence and start at 0; a document has at most 819 tokens.
All inputs are finite; a program needn't handle non-finite values.
Results may differ from the reference program's by a relative error of at most 0.013.
Values may be sent and summed in bfloat16 or wider, within the bound.
A program may use at most 384 MiB of HBM per device.

```python
import math
import jax
import jax.numpy as jnp
import numpy as np
from jax import lax

D = 768
H = 12
HD = 64
FF = 3072
SEQ = 2048
NSEQ = 8
TOKENS = 16384


def steps_of(key, shape, cuts, least, top_value):
    gain, own = 1.0, jax.random.fold_in(key, 6)
    for axis_at, parts in cuts:
        steps = jnp.exp(jax.random.uniform(jax.random.fold_in(own, axis_at), (parts,), jnp.float32, least / len(cuts), top_value / len(cuts)))
        gain = gain * jnp.repeat(steps, shape[axis_at] // parts).reshape([-1 if axis == axis_at else 1 for axis in range(len(shape))])
    return gain


def split_up(count, total, limit, slope):
    loads = [(1 << 20) // math.isqrt(rank ** slope) + 1 for rank in range(2, count + 1)]
    spare, counts = total - limit - (count - 1), [1] * (count - 1)
    while spare > 0:
        movable = [i for i in range(count - 1) if counts[i] < limit]
        whole, budget = sum([loads[i] for i in movable]), spare
        for i in movable:
            extra = min(limit - counts[i], max(1, budget * loads[i] // whole), spare)
            counts[i] = counts[i] + extra
            spare = spare - extra
    return np.array([limit] + counts)


def uneven_parts(own_key, count, total, limit, slope):
    if count == 2:
        one = jax.random.randint(own_key, (), max(1, total - limit), min(limit, total - 1) + 1)
        return jnp.stack([one, total - one])
    lengths = jnp.asarray(split_up(count, total, limit, slope), jnp.int32)
    twos = (count - 1) // 2
    giver, taker = lengths[1:1 + 2 * twos:2], lengths[2:2 + 2 * twos:2]
    slack = jnp.minimum(giver - 1, limit - taker)
    passed = jax.random.randint(jax.random.fold_in(own_key, 1), (twos,), 0, 1 << 20) % (slack + 1)
    lengths = lengths.at[1:1 + 2 * twos:2].set(giver - passed).at[2:2 + 2 * twos:2].set(taker + passed)
    return lengths[jax.random.permutation(jax.random.fold_in(own_key, 2), count)]


def scatter_about(key, shape, width, most, shards=(), kind=jnp.bfloat16):
    values = jax.random.normal(key, shape, jnp.float32) * width
    if len(shards) > 0:
        values = steps_of(key, shape, shards, -0.22, 0.18) * values
    return jnp.clip(values, min=-most, max=most).astype(kind)


def setup_inputs(seed: int = 0) -> dict:
    splits = jax.random.split(jax.random.key(seed), 19)
    return {
        "tokens": scatter_about(splits[0], (D, TOKENS), 1.0, 6.0, ((0, 4), (1, 8))),
        "segments": jax.vmap(lambda own: jnp.searchsorted(jnp.cumsum(uneven_parts(own, max(4, SEQ // 256), SEQ, SEQ * 2 // 5, 2)), jnp.arange(SEQ), side="right"))(jax.random.split(splits[1], NSEQ)).reshape((NSEQ, SEQ)).astype(jnp.int32),
        "ln1_gain": jnp.clip(1.0 + 0.12 * jax.random.normal(splits[2], (D,), jnp.float32), 0.3984375, 1.59375).astype(jnp.bfloat16),
        "ln1_bias": scatter_about(splits[3], (D,), 0.3, 1.75, ((0, 4),)),
        "w_query": scatter_about(splits[4], (D, D), D ** -0.5, 0.21875, ((0, 4), (1, 4))),
        "q_bias": scatter_about(splits[5], (D,), 0.3, 1.75, ((0, 4),)),
        "w_key": scatter_about(splits[6], (D, D), D ** -0.5, 0.21875, ((0, 4), (1, 4))),
        "w_value": scatter_about(splits[7], (D, D), D ** -0.5, 0.21875, ((0, 4), (1, 4))),
        "v_bias": scatter_about(splits[8], (D,), 0.3, 1.75, ((0, 4),)),
        "w_out": scatter_about(splits[9], (D, D), (D // 64) ** -0.5, 1.75, ((0, 4), (1, 4))),
        "out_bias": scatter_about(splits[10], (D,), 0.3, 1.75, ((0, 4),)),
        "ln2_gain": jnp.clip(1.0 + 0.12 * jax.random.normal(splits[11], (D,), jnp.float32), 0.3984375, 1.59375).astype(jnp.bfloat16),
        "ln2_bias": scatter_about(splits[12], (D,), 0.3, 1.75, ((0, 4),)),
        "w_up": scatter_about(splits[13], (D, FF), D ** -0.5, 0.21875, ((0, 4), (1, 4))),
        "up_bias": scatter_about(splits[14], (FF,), 0.3, 1.75, ((0, 4),)),
        "w_down": scatter_about(splits[15], (D, FF), FF ** -0.5, 0.109375, ((0, 4), (1, 4))),
        "down_bias": scatter_about(splits[16], (D,), 0.3, 1.75, ((0, 4),)),
        "cotangent": scatter_about(splits[17], (D, TOKENS), 1.0, 6.0, ((0, 4), (1, 8))),
    }


EPS = 1e-05
NEG = -1000000000.0
HIGH = lax.Precision.HIGHEST

@jax.custom_vjp
def low(v):
    return lax.optimization_barrier(v.astype(jnp.bfloat16)).astype(jnp.float32)

@jax.custom_vjp
def low_back(v):
    return v

def low_keep(v):
    return (low(v), None)

def low_pass(kept, grad):
    return (grad,)

def back_keep(v):
    return (v, None)

def back_low(kept, grad):
    return (low(grad),)
low.defvjp(low_keep, low_pass)
low_back.defvjp(back_keep, back_low)

def matmul(left_side, right_side):
    return jnp.dot(left_side, right_side, precision=HIGH, preferred_element_type=jnp.float32)

def layer_norm(values, norm_gain, norm_shift):
    center = lax.optimization_barrier(jnp.mean(values, axis=-1, keepdims=True))
    offset = values - center
    spread = lax.optimization_barrier(jnp.mean(offset * offset, axis=-1, keepdims=True))
    return offset * lax.rsqrt(spread + EPS) * norm_gain + norm_shift

def attend_sequence(operands):
    queries, keys_all, values_all, labels = operands
    length = queries.shape[0]
    block_rows = min(512, length)
    places = jnp.arange(length, dtype=jnp.int32)
    scale_factor = HD ** (-0.5)

    def one_block(number):
        row_start = number * block_rows
        block_query = lax.dynamic_slice_in_dim(queries, row_start, block_rows, 0)
        block_places = lax.dynamic_slice_in_dim(places, row_start, block_rows, 0)
        block_labels = lax.dynamic_slice_in_dim(labels, row_start, block_rows, 0)
        scores = jnp.einsum('qhd,khd->hqk', block_query, keys_all, precision=HIGH) * scale_factor
        scores = low_back(scores)
        allowed = (block_places[:, None] >= places[None, :]) & (block_labels[:, None] == labels[None, :])
        scores = jnp.where(allowed[None], scores, NEG)
        highest = lax.optimization_barrier(jnp.max(scores, axis=-1, keepdims=True))
        weights = jnp.exp(scores - highest)
        probability = weights / lax.optimization_barrier(jnp.sum(weights, axis=-1, keepdims=True))
        return jnp.einsum('hqk,khd->qhd', low(probability), values_all, precision=HIGH)
    blocks = lax.map(jax.checkpoint(one_block), jnp.arange(length // block_rows, dtype=jnp.int32))
    return blocks.reshape(queries.shape)

def forward(tokens, ln1_gain, ln1_bias, w_query, q_bias, w_key, w_value, v_bias, w_out, out_bias, ln2_gain, ln2_bias, w_up, up_bias, w_down, down_bias, segments):
    normed_a = low(layer_norm(tokens, ln1_gain, ln1_bias))
    query_rows = low(low_back(matmul(normed_a, w_query) + q_bias))
    key_rows = low(low_back(matmul(normed_a, w_key)))
    value_rows = low(low_back(matmul(normed_a, w_value) + v_bias))
    split_shape = (segments.shape[0], segments.shape[1], H, HD)
    attended = lax.map(attend_sequence, (query_rows.reshape(split_shape), key_rows.reshape(split_shape), value_rows.reshape(split_shape), segments))
    attended = low(low_back(attended.reshape(tokens.shape)))
    hidden = tokens + low_back(matmul(attended, w_out) + out_bias)
    normed_b = low(layer_norm(hidden, ln2_gain, ln2_bias))
    pre_act = low_back(matmul(normed_b, w_up) + up_bias)
    activated = low(jax.nn.gelu(pre_act))
    return hidden + low_back(matmul(activated, jnp.transpose(w_down)) + down_bias)

def reference(tokens, segments, ln1_gain, ln1_bias, w_query, q_bias, w_key, w_value, v_bias, w_out, out_bias, ln2_gain, ln2_bias, w_up, up_bias, w_down, down_bias, cotangent):
    token_rows = jnp.transpose(tokens.astype(jnp.float32))
    floats = (token_rows,) + tuple((operand.astype(jnp.float32) for operand in (ln1_gain, ln1_bias, w_query, q_bias, w_key, w_value, v_bias, w_out, out_bias, ln2_gain, ln2_bias, w_up, up_bias, w_down, down_bias)))

    def wrapped(*params):
        return forward(*params, segments)
    result, pull_back = jax.vjp(wrapped, *floats)
    gradients = pull_back(jnp.transpose(cotangent.astype(jnp.float32)))
    return (jnp.transpose(result).astype(jnp.bfloat16), jnp.transpose(gradients[0]), gradients[1], gradients[2], gradients[3], gradients[4], gradients[5], gradients[6], gradients[7], gradients[8], gradients[9], gradients[10], gradients[11], gradients[12], gradients[13], gradients[14], gradients[15])
```

```python
import functools

import jax
import jax.numpy as jnp
from jax import lax
from jax.experimental import pallas as pl
from jax.experimental.pallas import tpu as pltpu
from jax.sharding import PartitionSpec as P

HD = 64
EPS = 1e-05
NEG = -1000000000.0
BLOCK = 256
SCALE = HD ** (-0.5)
F32 = jnp.float32
BF16 = jnp.bfloat16


def contract(left, right, left_dim, right_dim):
    return lax.dot_general(
        left, right, (((left_dim,), (right_dim,)), ((), ())), preferred_element_type=F32
    )


def block_mask(query_block, key_block, query_labels, key_labels):
    shape = (BLOCK, BLOCK)
    key_places = key_block * BLOCK + lax.broadcasted_iota(jnp.int32, shape, 0)
    query_places = query_block * BLOCK + lax.broadcasted_iota(jnp.int32, shape, 1)
    return (query_places >= key_places) & (key_labels == query_labels)


def forward_kernel(heads, first_ref, seg_row, seg_col, q_ref, k_ref, v_ref, o_ref, lse_ref):
    i = pl.program_id(0)
    query_labels = seg_row[...]
    queries = [q_ref[h * HD : (h + 1) * HD, :] for h in range(heads)]

    def step(j, carried):
        start = pl.multiple_of(j * BLOCK, BLOCK)
        allowed = block_mask(i, j, query_labels, seg_col[pl.ds(start, BLOCK), :])
        after = []
        for h in range(heads):
            highest, total, acc = carried[h]
            scores = contract(k_ref[h, pl.ds(start, BLOCK), :], queries[h], 1, 0) * SCALE
            scores = jnp.where(allowed, scores, NEG)
            higher = jnp.maximum(highest, jnp.max(scores, 0, keepdims=True))
            shrink = jnp.exp(highest - higher)
            weights = jnp.exp(scores - higher)
            total = total * shrink + jnp.sum(weights, 0, keepdims=True)
            values = v_ref[h * HD : (h + 1) * HD, pl.ds(start, BLOCK)]
            acc = acc * shrink + contract(values, weights.astype(BF16), 1, 0)
            after.append((higher, total, acc))
        return tuple(after)

    empty = (
        jnp.full((1, BLOCK), NEG, F32),
        jnp.zeros((1, BLOCK), F32),
        jnp.zeros((HD, BLOCK), F32),
    )
    carried = lax.fori_loop(first_ref[i], i + 1, step, (empty,) * heads)
    lse_ref[...] = jnp.zeros_like(lse_ref)
    for h in range(heads):
        highest, total, acc = carried[h]
        o_ref[h * HD : (h + 1) * HD, :] = (acc / total).astype(BF16)
        lse_ref[h : h + 1, :] = highest + jnp.log(total)


def attend_forward(queries, key_rows, values, labels):
    width, length = queries.shape
    heads = width // HD
    starts = labels[::BLOCK]
    first = jnp.sum(labels[None, :] < starts[:, None], 1, dtype=jnp.int32) // BLOCK
    return pl.pallas_call(
        functools.partial(forward_kernel, heads),
        grid_spec=pltpu.PrefetchScalarGridSpec(
            num_scalar_prefetch=1,
            grid=(length // BLOCK,),
            in_specs=[
                pl.BlockSpec((1, BLOCK), lambda i, first: (0, i)),
                pl.BlockSpec((length, 1), lambda i, first: (0, 0)),
                pl.BlockSpec((width, BLOCK), lambda i, first: (0, i)),
                pl.BlockSpec((heads, length, HD), lambda i, first: (0, 0, 0)),
                pl.BlockSpec((width, length), lambda i, first: (0, 0)),
            ],
            out_specs=[
                pl.BlockSpec((width, BLOCK), lambda i, first: (0, i)),
                pl.BlockSpec((8, BLOCK), lambda i, first: (0, i)),
            ],
        ),
        out_shape=[
            jax.ShapeDtypeStruct((width, length), BF16),
            jax.ShapeDtypeStruct((8, length), F32),
        ],
        compiler_params=pltpu.CompilerParams(vmem_limit_bytes=40 * 2**20),
        cost_estimate=pl.CostEstimate(
            flops=2 * width * length * length, bytes_accessed=4 * 2 * width * length,
            transcendentals=heads * length * length // 2,
        ),
        name="attend_forward",
    )(first, labels[None, :], labels[:, None], queries, key_rows, values)


def backward_kernel(
    heads, last_ref, seg_row, seg_col, k_ref, v_ref, kt_ref, q_ref, g_ref, lse_ref, delta_ref,
    dq_ref, dk_ref, dv_ref, dq_sum,
):
    j = pl.program_id(0)
    key_labels = seg_col[...]

    @pl.when(j == 0)
    def _():
        dq_sum[...] = jnp.zeros_like(dq_sum)

    def step(i, carried):
        start = pl.multiple_of(i * BLOCK, BLOCK)
        span = pl.ds(start, BLOCK)
        allowed = block_mask(i, j, seg_row[:, span], key_labels)
        after = []
        for h in range(heads):
            dk, dv = carried[h]
            part = slice(h * HD, (h + 1) * HD)
            queries = q_ref[part, span]
            grads = g_ref[part, span]
            scores = contract(k_ref[h], queries, 1, 0) * SCALE
            probs = jnp.exp(jnp.where(allowed, scores - lse_ref[h : h + 1, span], NEG))
            grad_probs = contract(v_ref[h], grads, 1, 0)
            grad_scores = (probs * (grad_probs - delta_ref[h : h + 1, span])).astype(BF16)
            dv = dv + contract(grads, probs.astype(BF16), 1, 1)
            dk = dk + contract(queries, grad_scores, 1, 1)
            dq_sum[part, span] += contract(kt_ref[part, :], grad_scores, 1, 0)
            after.append((dk, dv))
        return tuple(after)

    zero = jnp.zeros((HD, BLOCK), F32)
    carried = lax.fori_loop(j, last_ref[j], step, ((zero, zero),) * heads)
    for h in range(heads):
        part = slice(h * HD, (h + 1) * HD)
        dk_ref[part, :] = (carried[h][0] * SCALE).astype(BF16)
        dv_ref[part, :] = carried[h][1].astype(BF16)

    @pl.when(j == pl.num_programs(0) - 1)
    def _():
        dq_ref[...] = (dq_sum[...] * SCALE).astype(BF16)


def attend_backward(queries, keys, key_rows, value_rows, grads, lse, delta, labels):
    width, length = queries.shape
    heads = width // HD
    ends = labels[BLOCK - 1 :: BLOCK]
    last = (
        jnp.sum(labels[None, :] <= ends[:, None], 1, dtype=jnp.int32) + BLOCK - 1
    ) // BLOCK
    rows = pl.BlockSpec((heads, BLOCK, HD), lambda j, last: (0, j, 0))
    whole = pl.BlockSpec((width, length), lambda j, last: (0, 0))
    piece = pl.BlockSpec((width, BLOCK), lambda j, last: (0, j))
    stats = pl.BlockSpec((8, length), lambda j, last: (0, 0))
    return pl.pallas_call(
        functools.partial(backward_kernel, heads),
        grid_spec=pltpu.PrefetchScalarGridSpec(
            num_scalar_prefetch=1,
            grid=(length // BLOCK,),
            in_specs=[
                pl.BlockSpec((1, length), lambda j, last: (0, 0)),
                pl.BlockSpec((BLOCK, 1), lambda j, last: (j, 0)),
                rows,
                rows,
                piece,
                whole,
                whole,
                stats,
                stats,
            ],
            out_specs=[whole, piece, piece],
            scratch_shapes=[pltpu.VMEM((width, length), F32)],
        ),
        out_shape=[jax.ShapeDtypeStruct((width, length), BF16)] * 3,
        compiler_params=pltpu.CompilerParams(vmem_limit_bytes=40 * 2**20),
        cost_estimate=pl.CostEstimate(
            flops=5 * width * length * length, bytes_accessed=8 * 2 * width * length,
            transcendentals=heads * length * length // 2,
        ),
        name="attend_backward",
    )(last, labels[None, :], labels[:, None], key_rows, value_rows, keys, queries, grads, lse, delta)


def head_rows(columns):
    return jnp.transpose(columns.reshape(-1, HD, columns.shape[1]), (0, 2, 1))


def swap(array, bit):
    count = lax.axis_size("row")
    return lax.ppermute(array, "row", [(place, place ^ bit) for place in range(count)])


def add_other_dp(array):
    return array.astype(F32) + lax.ppermute(array, "dp", [(0, 1), (1, 0)]).astype(F32)


def norm_stats(values):
    center = jnp.mean(values, 0, keepdims=True)
    offset = values - center
    return center, lax.rsqrt(jnp.mean(offset * offset, 0, keepdims=True) + EPS)


def own_block(full, place, width, axis):
    return lax.dynamic_slice_in_dim(full, place * width, width, axis)


def put_block(block, place, count):
    blank = jnp.zeros((block.shape[0] * count,), F32)
    return lax.dynamic_update_slice(blank, block, (place * block.shape[0],))


def local(
    tokens, segments, ln1_gain, ln1_bias, w_query, q_bias, w_key, w_value, v_bias, w_out,
    out_bias, ln2_gain, ln2_bias, w_up, up_bias, w_down, down_bias, cotangent,
):
    cols, rows = lax.axis_size("col"), lax.axis_size("row")
    length = segments.shape[1]
    held = tokens.shape[1]
    seqs = held // length
    group = cols // seqs
    own = held // cols
    features = tokens.shape[0]
    wide = features * cols
    block = w_query.shape[1]
    hidden_block = w_up.shape[1]
    r, c = lax.axis_index("row"), lax.axis_index("col")
    seq, place = c // group, c % group
    head = r ^ place
    groups = None
    if seqs > 1:
        groups = [[s * group + g for g in range(group)] for s in range(seqs)]
    mixed = [
        (a * cols + b, (a ^ (b % group)) * cols + b) for a in range(rows) for b in range(cols)
    ]

    vectors = jnp.stack([ln1_gain, ln1_bias, ln2_gain, ln2_bias, out_bias, down_bias], 1)
    first_pack = jnp.concatenate([w_query, w_key, w_value, vectors], 1)
    first_all = lax.all_gather(first_pack, "col", axis=0, tiled=True)
    x_all = lax.all_gather(tokens, "col", axis=0, tiled=True)
    w_joint = lax.ppermute(first_all[:, : 3 * block], ("row", "col"), mixed)
    vecs = first_all[:, 3 * block :].astype(F32)
    gain_one, shift_one, gain_two, shift_two, bias_out, bias_down = (
        vecs[:, n : n + 1] for n in range(6)
    )
    row_biases = lax.all_gather(jnp.concatenate([q_bias, v_bias, up_bias]), "row", axis=0)
    row_biases = row_biases.astype(F32)
    head_bias = lax.dynamic_index_in_dim(row_biases, head, 0, keepdims=False)
    joint_bias = jnp.concatenate(
        [head_bias[:block], jnp.zeros((block,), F32), head_bias[block : 2 * block]]
    )
    bias_up = jnp.concatenate(
        [
            lax.dynamic_index_in_dim(row_biases, who, 0, keepdims=False)[2 * block :]
            for who in (r, r ^ 2)
        ]
    )
    second_pack = jnp.concatenate([w_up, w_down, jnp.transpose(w_out)], 1)
    second_all = lax.all_gather(second_pack, "col", axis=0, tiled=True)
    up_down = second_all[:, : 2 * hidden_block]
    up_down_other = swap(up_down, 2)
    weight_up = jnp.concatenate(
        [up_down[:, :hidden_block], up_down_other[:, :hidden_block]], 1
    )
    weight_down = jnp.concatenate(
        [up_down[:, hidden_block:], up_down_other[:, hidden_block:]], 1
    )
    out_blocks = lax.all_gather(second_all[:, 2 * hidden_block :], "row", axis=0)
    weight_out = jnp.concatenate(
        [lax.dynamic_index_in_dim(out_blocks, r ^ g, 0, keepdims=False) for g in range(group)], 1
    )

    labels = lax.dynamic_index_in_dim(segments, r * seqs + seq, 0, keepdims=False)
    center_all, inverse_all = norm_stats(x_all.astype(F32))
    center = own_block(center_all, seq, length, 1)
    inverse = own_block(inverse_all, seq, length, 1)
    hat_a = (own_block(x_all, seq, length, 1).astype(F32) - center) * inverse
    normed_a = (hat_a * gain_one + shift_one).astype(BF16)
    joint = (contract(w_joint, normed_a, 0, 0) + joint_bias[:, None]).astype(BF16)
    queries, keys, values = joint[:block], joint[block : 2 * block], joint[2 * block :]
    key_rows, value_rows = head_rows(keys), head_rows(values)
    attended, lse = attend_forward(queries, key_rows, values, labels)

    att = lax.all_to_all(attended, "col", 1, 0, axis_index_groups=groups, tiled=True)
    ct_own = lax.all_to_all(cotangent, "col", 1, 0, tiled=True)
    ct_pair = jnp.concatenate([ct_own, swap(ct_own, 1)], 1)
    x_own = own_block(x_all, c, own, 1).astype(F32)
    hidden = x_own + contract(weight_out, att, 1, 0) + bias_out
    center_b, inverse_b = norm_stats(hidden)
    hat_b = (hidden - center_b) * inverse_b
    normed_b = (hat_b * gain_two + shift_two).astype(BF16)
    norm_pair = jnp.concatenate([normed_b, swap(normed_b, 1)], 1)
    pre_act = contract(weight_up, norm_pair, 0, 0) + bias_up[:, None]
    activated = jax.nn.gelu(pre_act).astype(BF16)
    down = contract(weight_down, activated, 1, 0)
    down = down[:, :own] + swap(down[:, own:].astype(BF16), 1).astype(F32)
    result = (hidden + down + bias_down).astype(BF16)
    out = lax.all_to_all(result, "col", 0, 1, tiled=True)

    grad_act = contract(weight_down, ct_pair, 0, 0)
    _, pull = jax.vjp(jax.nn.gelu, pre_act)
    grad_pre = pull(grad_act)[0].astype(BF16)
    grad_b = contract(weight_up, grad_pre, 1, 0)
    grad_b = grad_b[:, :own] + swap(grad_b[:, own:].astype(BF16), 1).astype(F32)
    scaled = grad_b * gain_two
    grad_hidden = ct_own.astype(F32) + inverse_b * (
        scaled
        - jnp.mean(scaled, 0, keepdims=True)
        - hat_b * jnp.mean(scaled * hat_b, 0, keepdims=True)
    )
    branch = grad_hidden.astype(BF16)
    grad_att = contract(weight_out, branch, 0, 0).astype(BF16)
    grad_att = lax.all_to_all(grad_att, "col", 0, 1, axis_index_groups=groups, tiled=True)
    hidden_cols = lax.all_to_all(branch, "col", 0, 1, tiled=True)

    down_grad = contract(ct_pair, activated, 1, 1)
    up_grad = contract(norm_pair, grad_pre, 1, 1)
    other = jnp.concatenate(
        [up_grad[:, hidden_block:].astype(BF16), down_grad[:, hidden_block:].astype(BF16)], 1
    )
    mine = jnp.concatenate([up_grad[:, :hidden_block], down_grad[:, :hidden_block]], 1)
    up_down_grad = (mine + swap(other, 2).astype(F32)).astype(BF16)
    out_grad = contract(branch, att, 1, 1).astype(BF16)
    out_grad = jnp.stack(
        [own_block(out_grad, r ^ h, block, 1) for h in range(rows)], 0
    )
    out_grad = lax.psum_scatter(out_grad, "row", scatter_dimension=0, tiled=False)
    second_grad = lax.psum_scatter(
        jnp.concatenate([up_down_grad, out_grad], 1), "col", scatter_dimension=0, tiled=True
    )
    second_grad = add_other_dp(second_grad)

    heads = block // HD
    delta = jnp.sum(
        (grad_att.astype(F32) * attended.astype(F32)).reshape(heads, HD, length), 1
    )
    delta = jnp.concatenate([delta, jnp.zeros((8 - heads, length), F32)], 0)
    grad_joint = jnp.concatenate(
        attend_backward(queries, keys, key_rows, value_rows, grad_att, lse, delta, labels), 0
    )
    grad_a = contract(w_joint, grad_joint, 1, 0)
    scaled_a = grad_a * gain_one
    sums = jnp.concatenate(
        [
            jnp.sum(scaled_a, 0, keepdims=True),
            jnp.sum(scaled_a * hat_a, 0, keepdims=True),
            jnp.zeros((14, length), F32),
        ],
        0,
    ).astype(BF16)
    sent = jnp.concatenate(
        [
            grad_a.astype(BF16).reshape(cols, features, length),
            jnp.broadcast_to(sums[None], (cols,) + sums.shape),
        ],
        1,
    )
    got = lax.all_to_all(sent, "col", 0, 0, tiled=True)
    got = jnp.sum(got.reshape(seqs, group, features + 16, length).astype(F32), 1)
    got = jnp.transpose(got, (1, 0, 2)).reshape(features + 16, held)
    grad_in = got[:features]
    hat_cols = (tokens.astype(F32) - center_all) * inverse_all
    grad_tokens = hidden_cols.astype(F32) + inverse_all * (
        grad_in * ln1_gain.astype(F32)[:, None]
        - got[features : features + 1] / wide
        - hat_cols * (got[features + 1 : features + 2] / wide)
    )

    joint_grad = contract(normed_a, grad_joint, 1, 1).astype(BF16)
    joint_grad = lax.ppermute(joint_grad, ("row", "col"), mixed)
    joint_grad = lax.psum_scatter(joint_grad, "col", scatter_dimension=0, tiled=True)
    joint_grad = add_other_dp(joint_grad)

    bias_sums = jnp.sum(grad_joint.astype(F32), 1)
    up_sums = jnp.sum(grad_pre.astype(F32), 1)
    small = jnp.concatenate(
        [
            put_block(jnp.sum(grad_in * hat_cols, 1), c, cols),
            put_block(jnp.sum(grad_in, 1), c, cols),
            put_block(jnp.sum(cotangent.astype(F32), 1), c, cols),
            jnp.sum(branch.astype(F32), 1),
            jnp.sum(grad_b * hat_b, 1),
            jnp.sum(grad_b, 1),
            put_block(bias_sums[:block], head, rows),
            put_block(bias_sums[2 * block :], head, rows),
            put_block(up_sums[:hidden_block], r, rows)
            + put_block(up_sums[hidden_block:], r ^ 2, rows),
        ]
    )
    small = lax.psum(small, ("dp", "row", "col"))
    by_col = [own_block(small[n * wide : (n + 1) * wide], c, features, 0) for n in range(6)]
    tail = small[6 * wide :]
    total_heads = block * rows
    q_sum = own_block(tail[:total_heads], r, block, 0)
    v_sum = own_block(tail[total_heads : 2 * total_heads], r, block, 0)
    up_sum = own_block(tail[2 * total_heads :], r, hidden_block, 0)
    return (
        out,
        grad_tokens,
        by_col[0],
        by_col[1],
        joint_grad[:, :block],
        q_sum,
        joint_grad[:, block : 2 * block],
        joint_grad[:, 2 * block :],
        v_sum,
        jnp.transpose(second_grad[:, 2 * hidden_block :]),
        by_col[3],
        by_col[4],
        by_col[5],
        second_grad[:, :hidden_block],
        up_sum,
        second_grad[:, hidden_block : 2 * hidden_block],
        by_col[2],
    )


def solution(mesh):
    placed = (
        P("col", ("dp", "row")),
        P("dp", None),
        P("col"),
        P("col"),
        P("col", "row"),
        P("row"),
        P("col", "row"),
        P("col", "row"),
        P("row"),
        P("row", "col"),
        P("col"),
        P("col"),
        P("col"),
        P("col", "row"),
        P("row"),
        P("col", "row"),
        P("col"),
        P("col", ("dp", "row")),
    )
    return jax.shard_map(
        local,
        mesh=mesh,
        in_specs=placed,
        out_specs=(
            P("col", ("dp", "row")),
            P("col", ("dp", "row")),
            P("col"),
            P("col"),
            P("col", "row"),
            P("row"),
            P("col", "row"),
            P("col", "row"),
            P("row"),
            P("row", "col"),
            P("col"),
            P("col"),
            P("col"),
            P("col", "row"),
            P("row"),
            P("col", "row"),
            P("col"),
        ),
        check_vma=False,
    )
```

```python
import functools

import jax
import jax.numpy as jnp
from jax import lax
from jax.experimental import pallas as pl
from jax.experimental.pallas import tpu as pltpu
from jax.sharding import PartitionSpec as P

HD = 64
EPS = 1e-05
NEG = -1000000000.0
BLOCK = 256
SCALE = HD ** (-0.5)
F32 = jnp.float32
BF16 = jnp.bfloat16


def contract(left, right, left_dim, right_dim):
    return lax.dot_general(
        left, right, (((left_dim,), (right_dim,)), ((), ())), preferred_element_type=F32
    )


def block_mask(query_block, key_block, query_labels, key_labels):
    shape = (BLOCK, BLOCK)
    key_places = key_block * BLOCK + lax.broadcasted_iota(jnp.int32, shape, 0)
    query_places = query_block * BLOCK + lax.broadcasted_iota(jnp.int32, shape, 1)
    return (query_places >= key_places) & (key_labels == query_labels)


def forward_kernel(heads, first_ref, seg_row, seg_col, q_ref, k_ref, v_ref, o_ref, lse_ref):
    i = pl.program_id(0)
    query_labels = seg_row[...]
    queries = [q_ref[h * HD : (h + 1) * HD, :] for h in range(heads)]

    def step(j, carried):
        start = pl.multiple_of(j * BLOCK, BLOCK)
        allowed = block_mask(i, j, query_labels, seg_col[pl.ds(start, BLOCK), :])
        after = []
        for h in range(heads):
            highest, total, acc = carried[h]
            scores = contract(k_ref[h, pl.ds(start, BLOCK), :], queries[h], 1, 0) * SCALE
            scores = jnp.where(allowed, scores, NEG)
            higher = jnp.maximum(highest, jnp.max(scores, 0, keepdims=True))
            shrink = jnp.exp(highest - higher)
            weights = jnp.exp(scores - higher)
            total = total * shrink + jnp.sum(weights, 0, keepdims=True)
            values = v_ref[h * HD : (h + 1) * HD, pl.ds(start, BLOCK)]
            acc = acc * shrink + contract(values, weights.astype(BF16), 1, 0)
            after.append((higher, total, acc))
        return tuple(after)

    empty = (
        jnp.full((1, BLOCK), NEG, F32),
        jnp.zeros((1, BLOCK), F32),
        jnp.zeros((HD, BLOCK), F32),
    )
    carried = lax.fori_loop(first_ref[i], i + 1, step, (empty,) * heads)
    lse_ref[...] = jnp.zeros_like(lse_ref)
    for h in range(heads):
        highest, total, acc = carried[h]
        o_ref[h * HD : (h + 1) * HD, :] = (acc / total).astype(BF16)
        lse_ref[h : h + 1, :] = highest + jnp.log(total)


def attend_forward(queries, key_rows, values, labels):
    width, length = queries.shape
    heads = width // HD
    starts = labels[::BLOCK]
    first = jnp.sum(labels[None, :] < starts[:, None], 1, dtype=jnp.int32) // BLOCK
    return pl.pallas_call(
        functools.partial(forward_kernel, heads),
        grid_spec=pltpu.PrefetchScalarGridSpec(
            num_scalar_prefetch=1,
            grid=(length // BLOCK,),
            in_specs=[
                pl.BlockSpec((1, BLOCK), lambda i, first: (0, i)),
                pl.BlockSpec((length, 1), lambda i, first: (0, 0)),
                pl.BlockSpec((width, BLOCK), lambda i, first: (0, i)),
                pl.BlockSpec((heads, length, HD), lambda i, first: (0, 0, 0)),
                pl.BlockSpec((width, length), lambda i, first: (0, 0)),
            ],
            out_specs=[
                pl.BlockSpec((width, BLOCK), lambda i, first: (0, i)),
                pl.BlockSpec((8, BLOCK), lambda i, first: (0, i)),
            ],
        ),
        out_shape=[
            jax.ShapeDtypeStruct((width, length), BF16),
            jax.ShapeDtypeStruct((8, length), F32),
        ],
        compiler_params=pltpu.CompilerParams(vmem_limit_bytes=40 * 2**20),
        cost_estimate=pl.CostEstimate(
            flops=24 * width * length * length, bytes_accessed=4 * 2 * width * length,
            transcendentals=heads * length * length // 2,
        ),
        name="attend_forward",
    )(first, labels[None, :], labels[:, None], queries, key_rows, values)


def backward_kernel(
    heads, last_ref, seg_row, seg_col, k_ref, v_ref, kt_ref, q_ref, g_ref, lse_ref, delta_ref,
    dq_ref, dk_ref, dv_ref, dq_sum,
):
    j = pl.program_id(0)
    key_labels = seg_col[...]

    @pl.when(j == 0)
    def _():
        dq_sum[...] = jnp.zeros_like(dq_sum)

    def step(i, carried):
        start = pl.multiple_of(i * BLOCK, BLOCK)
        span = pl.ds(start, BLOCK)
        allowed = block_mask(i, j, seg_row[:, span], key_labels)
        after = []
        for h in range(heads):
            dk, dv = carried[h]
            part = slice(h * HD, (h + 1) * HD)
            queries = q_ref[part, span]
            grads = g_ref[part, span]
            scores = contract(k_ref[h], queries, 1, 0) * SCALE
            probs = jnp.exp(jnp.where(allowed, scores - lse_ref[h : h + 1, span], NEG))
            grad_probs = contract(v_ref[h], grads, 1, 0)
            grad_scores = (probs * (grad_probs - delta_ref[h : h + 1, span])).astype(BF16)
            dv = dv + contract(grads, probs.astype(BF16), 1, 1)
            dk = dk + contract(queries, grad_scores, 1, 1)
            dq_sum[part, span] += contract(kt_ref[part, :], grad_scores, 1, 0)
            after.append((dk, dv))
        return tuple(after)

    zero = jnp.zeros((HD, BLOCK), F32)
    carried = lax.fori_loop(j, last_ref[j], step, ((zero, zero),) * heads)
    for h in range(heads):
        part = slice(h * HD, (h + 1) * HD)
        dk_ref[part, :] = (carried[h][0] * SCALE).astype(BF16)
        dv_ref[part, :] = carried[h][1].astype(BF16)

    @pl.when(j == pl.num_programs(0) - 1)
    def _():
        dq_ref[...] = (dq_sum[...] * SCALE).astype(BF16)


def attend_backward(queries, keys, key_rows, value_rows, grads, lse, delta, labels):
    width, length = queries.shape
    heads = width // HD
    ends = labels[BLOCK - 1 :: BLOCK]
    last = (
        jnp.sum(labels[None, :] <= ends[:, None], 1, dtype=jnp.int32) + BLOCK - 1
    ) // BLOCK
    rows = pl.BlockSpec((heads, BLOCK, HD), lambda j, last: (0, j, 0))
    whole = pl.BlockSpec((width, length), lambda j, last: (0, 0))
    piece = pl.BlockSpec((width, BLOCK), lambda j, last: (0, j))
    stats = pl.BlockSpec((8, length), lambda j, last: (0, 0))
    return pl.pallas_call(
        functools.partial(backward_kernel, heads),
        grid_spec=pltpu.PrefetchScalarGridSpec(
            num_scalar_prefetch=1,
            grid=(length // BLOCK,),
            in_specs=[
                pl.BlockSpec((1, length), lambda j, last: (0, 0)),
                pl.BlockSpec((BLOCK, 1), lambda j, last: (j, 0)),
                rows,
                rows,
                piece,
                whole,
                whole,
                stats,
                stats,
            ],
            out_specs=[whole, piece, piece],
            scratch_shapes=[pltpu.VMEM((width, length), F32)],
        ),
        out_shape=[jax.ShapeDtypeStruct((width, length), BF16)] * 3,
        compiler_params=pltpu.CompilerParams(vmem_limit_bytes=40 * 2**20),
        cost_estimate=pl.CostEstimate(
            flops=28 * width * length * length, bytes_accessed=8 * 2 * width * length,
            transcendentals=heads * length * length // 2,
        ),
        name="attend_backward",
    )(last, labels[None, :], labels[:, None], key_rows, value_rows, keys, queries, grads, lse, delta)


def head_rows(columns):
    return jnp.transpose(columns.reshape(-1, HD, columns.shape[1]), (0, 2, 1))


def swap(array, bit):
    count = lax.axis_size("row")
    return lax.ppermute(array, "row", [(place, place ^ bit) for place in range(count)])


def cross_dp(array):
    return lax.ppermute(array, "dp", [(0, 1), (1, 0)])


def half_pair(array, side):
    width = array.shape[1] // 2
    low, high = array[:, :width], array[:, width:]
    return jnp.where(side == 0, low, high), jnp.where(side == 0, high, low)


def halve_dp(array, side):
    kept, given = half_pair(array, side)
    return kept + cross_dp(given.astype(BF16)).astype(F32)


def join_dp(array, side):
    other = cross_dp(array)
    low = jnp.where(side == 0, array, other)
    high = jnp.where(side == 0, other, array)
    return jnp.concatenate([low, high], 1).astype(F32)


def norm_stats(values):
    center = jnp.mean(values, 0, keepdims=True)
    offset = values - center
    return center, lax.rsqrt(jnp.mean(offset * offset, 0, keepdims=True) + EPS)


def own_block(full, place, width, axis):
    return lax.dynamic_slice_in_dim(full, place * width, width, axis)


def put_block(block, place, count):
    blank = jnp.zeros((block.shape[0] * count,), F32)
    return lax.dynamic_update_slice(blank, block, (place * block.shape[0],))


def local(
    tokens, segments, ln1_gain, ln1_bias, w_query, q_bias, w_key, w_value, v_bias, w_out,
    out_bias, ln2_gain, ln2_bias, w_up, up_bias, w_down, down_bias, cotangent,
):
    cols, rows = lax.axis_size("col"), lax.axis_size("row")
    length = segments.shape[1]
    held = tokens.shape[1]
    seqs = held // length
    group = cols // seqs
    own = held // cols
    features = tokens.shape[0]
    wide = features * cols
    block = w_query.shape[1]
    hidden_block = w_up.shape[1]
    r, c = lax.axis_index("row"), lax.axis_index("col")
    seq, place = c // group, c % group
    head = r ^ place
    groups = None
    if seqs > 1:
        groups = [[s * group + g for g in range(group)] for s in range(seqs)]
    mixed = [
        (a * cols + b, (a ^ (b % group)) * cols + b) for a in range(rows) for b in range(cols)
    ]

    vectors = jnp.stack([ln1_gain, ln1_bias, ln2_gain, ln2_bias, out_bias, down_bias], 1)
    first_pack = jnp.concatenate([w_query, w_key, w_value, vectors], 1)
    first_all = lax.all_gather(first_pack, "col", axis=0, tiled=True)
    x_all = lax.all_gather(tokens, "col", axis=0, tiled=True)
    w_joint = lax.ppermute(first_all[:, : 3 * block], ("row", "col"), mixed)
    vecs = first_all[:, 3 * block :].astype(F32)
    gain_one, shift_one, gain_two, shift_two, bias_out, bias_down = (
        vecs[:, n : n + 1] for n in range(6)
    )
    row_biases = lax.all_gather(jnp.concatenate([q_bias, v_bias, up_bias]), "row", axis=0)
    row_biases = row_biases.astype(F32)
    head_bias = lax.dynamic_index_in_dim(row_biases, head, 0, keepdims=False)
    joint_bias = jnp.concatenate(
        [head_bias[:block], jnp.zeros((block,), F32), head_bias[block : 2 * block]]
    )
    bias_up = jnp.concatenate(
        [
            lax.dynamic_index_in_dim(row_biases, who, 0, keepdims=False)[2 * block :]
            for who in (r, r ^ 2)
        ]
    )
    second_pack = jnp.concatenate([w_up, w_down, jnp.transpose(w_out)], 1)
    second_pack, x_all = lax.optimization_barrier((second_pack, x_all))
    second_all = lax.all_gather(second_pack, "col", axis=0, tiled=True)
    up_down = second_all[:, : 2 * hidden_block]
    up_down_other = swap(up_down, 2)
    weight_up = jnp.concatenate(
        [up_down[:, :hidden_block], up_down_other[:, :hidden_block]], 1
    )
    weight_down = jnp.concatenate(
        [up_down[:, hidden_block:], up_down_other[:, hidden_block:]], 1
    )
    out_blocks = lax.all_gather(second_all[:, 2 * hidden_block :], "row", axis=0)
    weight_out = jnp.concatenate(
        [lax.dynamic_index_in_dim(out_blocks, r ^ g, 0, keepdims=False) for g in range(group)], 1
    )

    labels = lax.dynamic_index_in_dim(segments, r * seqs + seq, 0, keepdims=False)
    center_all, inverse_all = norm_stats(x_all.astype(F32))
    center = own_block(center_all, seq, length, 1)
    inverse = own_block(inverse_all, seq, length, 1)
    hat_a = (own_block(x_all, seq, length, 1).astype(F32) - center) * inverse
    normed_a = (hat_a * gain_one + shift_one).astype(BF16)
    joint = (contract(w_joint, normed_a, 0, 0) + joint_bias[:, None]).astype(BF16)
    queries, keys, values = joint[:block], joint[block : 2 * block], joint[2 * block :]
    key_rows, value_rows = head_rows(keys), head_rows(values)
    attended, lse = attend_forward(queries, key_rows, values, labels)

    att = lax.all_to_all(attended, "col", 1, 0, axis_index_groups=groups, tiled=True)
    ct_own = lax.all_to_all(cotangent, "col", 1, 0, tiled=True)
    ct_pair = jnp.concatenate([ct_own, swap(ct_own, 1)], 1)
    x_own = own_block(x_all, c, own, 1).astype(F32)
    hidden = x_own + contract(weight_out, att, 1, 0) + bias_out
    center_b, inverse_b = norm_stats(hidden)
    hat_b = (hidden - center_b) * inverse_b
    normed_b = (hat_b * gain_two + shift_two).astype(BF16)
    norm_pair = jnp.concatenate([normed_b, swap(normed_b, 1)], 1)
    pre_act = contract(weight_up, norm_pair, 0, 0) + bias_up[:, None]
    activated = jax.nn.gelu(pre_act).astype(BF16)
    down = contract(weight_down, activated, 1, 0)
    down = down[:, :own] + swap(down[:, own:].astype(BF16), 1).astype(F32)
    result = (hidden + down + bias_down).astype(BF16)
    out = lax.all_to_all(result, "col", 0, 1, tiled=True)

    grad_act = contract(weight_down, ct_pair, 0, 0)
    _, pull = jax.vjp(jax.nn.gelu, pre_act)
    grad_pre = pull(grad_act)[0].astype(BF16)
    grad_b = contract(weight_up, grad_pre, 1, 0)
    grad_b = grad_b[:, :own] + swap(grad_b[:, own:].astype(BF16), 1).astype(F32)
    scaled = grad_b * gain_two
    grad_hidden = ct_own.astype(F32) + inverse_b * (
        scaled
        - jnp.mean(scaled, 0, keepdims=True)
        - hat_b * jnp.mean(scaled * hat_b, 0, keepdims=True)
    )
    branch = grad_hidden.astype(BF16)
    grad_att = contract(weight_out, branch, 0, 0).astype(BF16)
    grad_att = lax.all_to_all(grad_att, "col", 0, 1, axis_index_groups=groups, tiled=True)
    hidden_cols = lax.all_to_all(branch, "col", 0, 1, tiled=True)

    down_grad = contract(ct_pair, activated, 1, 1)
    up_grad = contract(norm_pair, grad_pre, 1, 1)
    side = lax.axis_index("dp")
    kept_own, given_own = half_pair(up_grad[:, :hidden_block], side)
    kept_far, given_far = half_pair(up_grad[:, hidden_block:], side)
    given = cross_dp(jnp.concatenate([given_own, given_far], 1).astype(BF16)).astype(F32)
    half = hidden_block // 2
    up_far = swap((kept_far + given[:, half:]).astype(BF16), 2).astype(F32)
    up_half = (kept_own + given[:, :half] + up_far).astype(BF16)
    down_far = swap(down_grad[:, hidden_block:].astype(BF16), 2).astype(F32)
    down_half = halve_dp(down_grad[:, :hidden_block] + down_far, side).astype(BF16)
    out_grad = contract(branch, att, 1, 1).astype(BF16)
    out_grad = jnp.stack([own_block(out_grad, r ^ h, block, 1) for h in range(rows)], 0)
    out_grad = lax.all_to_all(out_grad, "row", 0, 0, tiled=True)
    out_grad, grad_att = lax.optimization_barrier((out_grad, grad_att))
    out_grad = jnp.sum(out_grad.astype(F32), 0).astype(BF16)
    out_grad = (out_grad.astype(F32) + cross_dp(out_grad).astype(F32)).astype(BF16)
    second_grad = lax.psum_scatter(
        jnp.concatenate([up_half, down_half, out_grad], 1), "col", scatter_dimension=0, tiled=True
    )
    grad_w_up = join_dp(second_grad[:, :half], side)
    grad_w_down = join_dp(second_grad[:, half : 2 * half], side)
    grad_w_out = jnp.transpose(second_grad[:, 2 * half :].astype(F32))

    heads = block // HD
    delta = jnp.sum(
        (grad_att.astype(F32) * attended.astype(F32)).reshape(heads, HD, length), 1
    )
    delta = jnp.concatenate([delta, jnp.zeros((8 - heads, length), F32)], 0)
    grad_joint = jnp.concatenate(
        attend_backward(queries, keys, key_rows, value_rows, grad_att, lse, delta, labels), 0
    )
    grad_a = contract(w_joint, grad_joint, 1, 0)
    scaled_a = grad_a * gain_one
    sums = jnp.concatenate(
        [
            jnp.sum(scaled_a, 0, keepdims=True),
            jnp.sum(scaled_a * hat_a, 0, keepdims=True),
            jnp.zeros((14, length), F32),
        ],
        0,
    ).astype(BF16)
    sent = jnp.concatenate(
        [
            grad_a.astype(BF16).reshape(cols, features, length),
            jnp.broadcast_to(sums[None], (cols,) + sums.shape),
        ],
        1,
    )
    got = lax.all_to_all(sent, "col", 0, 0, tiled=True)
    got = jnp.sum(got.reshape(seqs, group, features + 16, length).astype(F32), 1)
    got = jnp.transpose(got, (1, 0, 2)).reshape(features + 16, held)
    grad_in = got[:features]
    hat_cols = (tokens.astype(F32) - center_all) * inverse_all
    grad_tokens = hidden_cols.astype(F32) + inverse_all * (
        grad_in * ln1_gain.astype(F32)[:, None]
        - got[features : features + 1] / wide
        - hat_cols * (got[features + 1 : features + 2] / wide)
    )

    joint_grad = halve_dp(contract(normed_a, grad_joint, 1, 1), side).astype(BF16)
    joint_grad = lax.ppermute(joint_grad, ("row", "col"), mixed)
    joint_grad = lax.psum_scatter(joint_grad, "col", scatter_dimension=0, tiled=True)
    joint_grad = join_dp(joint_grad, side)

    bias_sums = jnp.sum(grad_joint.astype(F32), 1)
    up_sums = jnp.sum(grad_pre.astype(F32), 1)
    small = jnp.concatenate(
        [
            jnp.sum(grad_a * hat_a, 1),
            jnp.sum(grad_a, 1),
            put_block(jnp.sum(cotangent.astype(F32), 1), c, cols),
            jnp.sum(branch.astype(F32), 1),
            jnp.sum(grad_b * hat_b, 1),
            jnp.sum(grad_b, 1),
            put_block(bias_sums[:block], head, rows),
            put_block(bias_sums[2 * block :], head, rows),
            put_block(up_sums[:hidden_block], r, rows)
            + put_block(up_sums[hidden_block:], r ^ 2, rows),
        ]
    )
    small = lax.psum(small, ("dp", "row", "col"))
    by_col = [own_block(small[n * wide : (n + 1) * wide], c, features, 0) for n in range(6)]
    tail = small[6 * wide :]
    total_heads = block * rows
    q_sum = own_block(tail[:total_heads], r, block, 0)
    v_sum = own_block(tail[total_heads : 2 * total_heads], r, block, 0)
    up_sum = own_block(tail[2 * total_heads :], r, hidden_block, 0)
    return (
        out,
        grad_tokens,
        by_col[0],
        by_col[1],
        joint_grad[:, :block],
        q_sum,
        joint_grad[:, block : 2 * block],
        joint_grad[:, 2 * block :],
        v_sum,
        grad_w_out,
        by_col[3],
        by_col[4],
        by_col[5],
        grad_w_up,
        up_sum,
        grad_w_down,
        by_col[2],
    )


def solution(mesh):
    placed = (
        P("col", ("dp", "row")),
        P("dp", None),
        P("col"),
        P("col"),
        P("col", "row"),
        P("row"),
        P("col", "row"),
        P("col", "row"),
        P("row"),
        P("row", "col"),
        P("col"),
        P("col"),
        P("col"),
        P("col", "row"),
        P("row"),
        P("col", "row"),
        P("col"),
        P("col", ("dp", "row")),
    )
    return jax.shard_map(
        local,
        mesh=mesh,
        in_specs=placed,
        out_specs=(
            P("col", ("dp", "row")),
            P("col", ("dp", "row")),
            P("col"),
            P("col"),
            P("col", "row"),
            P("row"),
            P("col", "row"),
            P("col", "row"),
            P("row"),
            P("row", "col"),
            P("col"),
            P("col"),
            P("col"),
            P("col", "row"),
            P("row"),
            P("col", "row"),
            P("col"),
        ),
        check_vma=False,
    )
```
